32 devices in a mesh: ctx: 8 (over z, x), dp: 4 (over y, core).
Axes of the slice: x: 2, y: 2, z: 4, core: 2. Of those that a mesh axis runs over, the one named last changes fastest.
Arguments:
- query: bfloat16 [4, 2048, 512], P('dp', 'ctx'), may hold values from -170 to 170
- key: bfloat16 [4, 2048, 128], P('dp', 'ctx'), may hold values from -6.1 to 6.1
- value: bfloat16 [4, 2048, 128], P('dp', 'ctx'), may hold values from -6 to 6
- out_grad: bfloat16 [4, 2048, 512], P('dp', 'ctx'), may hold values from -6 to 6
- output: bfloat16 [4, 2048, 512], P('dp', 'ctx'), may hold values from -6 to 6
- inputs: bfloat16 [4, 2048, 8192], P('dp', 'ctx'), may hold values from -6 to 6
- span_ids: int32 [16], P('ctx'), may hold values from 0 to 15, each once
Outputs:
- query_grad: bfloat16 [4, 2048, 512], P('dp', 'ctx')
- key_grad: bfloat16 [4, 2048, 128], P('dp', 'ctx')
- value_grad: bfloat16 [4, 2048, 128], P('dp', 'ctx')
- grad_weights: float32 [8192, 256], replicated
The draws below stay inside these ranges and needn't reach their ends.
All inputs are finite; a program needn't handle non-finite values.
Results may differ from the reference program's by a relative error of at most 0.0054.
Values may be sent and summed in bfloat16 or wider, within the bound.
A program may use at most 64 MiB of HBM per device.

```python
import jax
import jax.numpy as jnp
from jax import lax

D = 8192
HD = 128
HEADS = 4
TOK_DEV = 256
SPAN = 128
SEQ = 2048
BATCH = 4
N_CTX = 8


def shared_rows(key):
    return jnp.clip(jax.random.normal(jax.random.fold_in(key, 101), (BATCH, SEQ, HD), jnp.float32), -6.0, 6.0)


def draw_key(key, part):
    rows = shared_rows(key)
    return rows.astype(jnp.bfloat16)


def draw_query(key, part):
    key = jax.random.fold_in(key, 13)
    result = jnp.clip(jax.random.normal(key, (BATCH, SEQ, HEADS, HD), jnp.float32), -6.0, 6.0)
    return result.reshape(BATCH, SEQ, HEADS * HD).astype(jnp.bfloat16)


def level_of(own_key, extent, shards, low, top_value):
    loudness, own = 1.0, jax.random.fold_in(own_key, 6)
    for dim, shards_of in shards:
        draws = jnp.exp(jax.random.uniform(jax.random.fold_in(own, dim), (shards_of,), jnp.float32, low / len(shards), top_value / len(shards)))
        loudness = loudness * jnp.repeat(draws, extent[dim] // shards_of).reshape([-1 if axis == dim else 1 for axis in range(len(extent))])
    return loudness


def noise(key, dims, deviation, most, split=(), held_as=jnp.bfloat16):
    values = deviation * jax.random.normal(key, dims, jnp.float32)
    if split:
        values = values * level_of(key, dims, split, -0.22, 0.18)
    return jnp.clip(values, -most, most).astype(held_as)


def setup_inputs(seed: int = 0) -> dict:
    splits = jax.random.split(jax.random.key(seed), 8)
    query = draw_query(jax.random.fold_in(splits[7], 71), 0)
    key = draw_key(jax.random.fold_in(splits[7], 71), 0)
    value = noise(splits[2], (BATCH, SEQ, HD), 1.0, 6.0, ((0, 4), (1, 8)))
    out_grad = noise(splits[3], (BATCH, SEQ, HEADS * HD), 1.0, 6.0, ((0, 4), (1, 8)))
    output = noise(splits[4], (BATCH, SEQ, HEADS * HD), 1.0, 6.0, ((0, 4), (1, 8)))
    inputs = noise(splits[5], (BATCH, SEQ, D), 1.0, 6.0, ((0, 4), (1, 8)))
    span_ids = jax.random.permutation(splits[6], 2 * N_CTX).astype(jnp.int32)
    return dict(query=query, key=key, value=value, out_grad=out_grad, output=output, inputs=inputs, span_ids=span_ids)


def reference(query, key, value, out_grad, output, inputs, span_ids):
    offsets = jnp.arange(SEQ, dtype=jnp.int32)
    position = (span_ids[offsets // SPAN] * SPAN + offsets % SPAN).astype(jnp.int32)
    score_scale = HD ** -0.5
    block_rows = TOK_DEV
    block_count = SEQ // block_rows
    query_list = []
    key_list = []
    value_list = []
    grad_weights = jnp.zeros((D, 2 * HD), jnp.float32)
    for batch_row in range(BATCH):
        keys_full = key[batch_row].astype(jnp.float32)
        values_full = value[batch_row].astype(jnp.float32)
        query_blocks = query[batch_row].astype(jnp.float32).reshape(block_count, block_rows, HEADS, HD)
        grad_blocks = out_grad[batch_row].astype(jnp.float32).reshape(block_count, block_rows, HEADS, HD)
        output_blocks = output[batch_row].astype(jnp.float32).reshape(block_count, block_rows, HEADS, HD)
        position_blocks = position.reshape(block_count, block_rows)

        def one_block(sums, pieces):
            query_here, grad_here, output_here, position_here = pieces
            visible = position[None, None, :] <= position_here[None, :, None]
            scores = jnp.einsum("rhe,ke->hrk", query_here, keys_full) * score_scale
            masked = jnp.where(visible, scores, -1e30)
            running_max = jnp.max(masked, axis=-1)
            lse = running_max + jnp.log(jnp.sum(jnp.where(visible, jnp.exp(masked - running_max[:, :, None]), 0.0), axis=-1))
            probs = jnp.where(visible, jnp.exp(scores - lse[:, :, None]), 0.0)
            prob_grads = jnp.einsum("rhe,ke->hrk", grad_here, values_full)
            delta = jnp.transpose(jnp.sum(grad_here * output_here, axis=-1))
            score_grads = (probs * (prob_grads - delta[:, :, None]) * score_scale).astype(jnp.bfloat16)
            score_grads = lax.optimization_barrier(score_grads).astype(jnp.float32)
            probs_low = lax.optimization_barrier(probs.astype(jnp.bfloat16)).astype(jnp.float32)
            query_part = jnp.einsum("hrk,ke->rhe", score_grads, keys_full)
            key_sum = sums[0] + jnp.einsum("hrk,rhe->ke", score_grads, query_here)
            value_sum = sums[1] + jnp.einsum("hrk,rhe->ke", probs_low, grad_here)
            return (key_sum, value_sum), query_part

        start_sums = (jnp.zeros((SEQ, HD), jnp.float32), jnp.zeros((SEQ, HD), jnp.float32))
        (key_sum, value_sum), query_parts = lax.scan(one_block, start_sums, (query_blocks, grad_blocks, output_blocks, position_blocks))
        key_low = key_sum.astype(jnp.bfloat16)
        value_low = value_sum.astype(jnp.bfloat16)
        query_list.append(query_parts.reshape(SEQ, HEADS * HD).astype(jnp.bfloat16))
        key_list.append(key_low)
        value_list.append(value_low)
        grad_pair = jnp.concatenate([key_low, value_low], axis=1)
        grad_weights = grad_weights + jnp.dot(inputs[batch_row].T, grad_pair, preferred_element_type=jnp.float32)
    return jnp.stack(query_list), jnp.stack(key_list), jnp.stack(value_list), grad_weights
```

```python
import functools

import jax
import jax.numpy as jnp
from jax import lax
from jax.experimental import pallas as pl
from jax.experimental.pallas import tpu as pltpu
from jax.sharding import PartitionSpec as P

NEG_FILL = -1e30
LOG2_E = 1.4426950408889634


def dot_nt(left, right):
    return lax.dot_general(left, right, (((1,), (1,)), ((), ())), preferred_element_type=jnp.float32)


def dot_nn(left, right):
    return lax.dot_general(left, right, (((1,), (0,)), ((), ())), preferred_element_type=jnp.float32)


def dot_tn(left, right):
    return lax.dot_general(left, right, (((0,), (0,)), ((), ())), preferred_element_type=jnp.float32)


def attention_kernel(
    chunks, heads, width, block,
    table_ref, own_ref, q_ref, g_ref, o_ref, kv_ref,
    dq_ref, dkv_ref, s_ref, acc_ref,
):
    rows = heads * block
    tokens = 2 * block
    scale = width ** -0.5
    key_row = lax.broadcasted_iota(jnp.int32, (block, rows), 0)
    query_col = lax.rem(lax.broadcasted_iota(jnp.int32, (block, rows), 1), block)
    gap = key_row - query_col
    for slot in range(2):

        def stacked(ref):
            part = ref[slot * block:(slot + 1) * block, :]
            return jnp.concatenate([part[:, h * width:(h + 1) * width] for h in range(heads)], axis=0)

        queries, grads = stacked(q_ref), stacked(g_ref)
        product = grads.astype(jnp.float32) * stacked(o_ref).astype(jnp.float32)
        delta = jnp.sum(jnp.transpose(product), axis=0, keepdims=True) * scale
        own = own_ref[slot]

        def score_step(chunk, high):
            base = pl.multiple_of(chunk * tokens, tokens)
            scores = dot_nt(kv_ref[pl.ds(base, tokens), :width], queries) * (scale * LOG2_E)
            for half in range(2):
                ahead = (own - table_ref[2 * chunk + half]) * block
                piece = jnp.where(gap <= ahead, scores[half * block:(half + 1) * block, :], NEG_FILL)
                s_ref[pl.ds(pl.multiple_of(base + half * block, block), block), :] = piece
                high = jnp.maximum(high, jnp.max(piece.reshape(block // 8, 8, rows), axis=0))
            return high

        high = lax.fori_loop(0, chunks, score_step, jnp.full((8, rows), NEG_FILL, jnp.float32))
        top = jnp.max(high, axis=0, keepdims=True)

        def exp_step(chunk, total):
            at = pl.ds(pl.multiple_of(chunk * tokens, tokens), tokens)
            weights = jnp.exp2(s_ref[at, :] - top)
            s_ref[at, :] = weights
            return total + jnp.sum(weights.reshape(tokens // 8, 8, rows), axis=0)

        total = lax.fori_loop(0, chunks, exp_step, jnp.zeros((8, rows), jnp.float32))
        inverse = 1.0 / jnp.sum(total, axis=0, keepdims=True)

        def grad_step(chunk, query_sum):
            at = pl.ds(pl.multiple_of(chunk * tokens, tokens), tokens)
            keys, values = kv_ref[at, :width], kv_ref[at, width:]
            probs = s_ref[at, :] * inverse
            prob_grads = dot_nt(values, grads)
            score_grads = (probs * (prob_grads * scale - delta)).astype(jnp.bfloat16)
            value_add = dot_nn(probs.astype(jnp.bfloat16), grads)
            key_add = dot_nn(score_grads, queries)
            if slot == 0:
                acc_ref[at, :width] = key_add
                acc_ref[at, width:] = value_add
            else:
                dkv_ref[at, :width] = (acc_ref[at, :width] + key_add).astype(jnp.bfloat16)
                dkv_ref[at, width:] = (acc_ref[at, width:] + value_add).astype(jnp.bfloat16)
            return query_sum + dot_tn(keys, score_grads)

        query_sum = lax.fori_loop(0, chunks, grad_step, jnp.zeros((width, rows), jnp.float32))
        for h in range(heads):
            dq_ref[slot * block:(slot + 1) * block, h * width:(h + 1) * width] = jnp.transpose(
                query_sum[:, h * block:(h + 1) * block]
            ).astype(jnp.bfloat16)


def attention(table, own, query, out_grad, output, key_value, width):
    tokens_dev, wide = query.shape
    length = key_value.shape[0]
    block = tokens_dev // 2
    heads = wide // width
    smem = pl.BlockSpec(memory_space=pltpu.SMEM)
    vmem = pl.BlockSpec(memory_space=pltpu.VMEM)
    return pl.pallas_call(
        functools.partial(attention_kernel, length // tokens_dev, heads, width, block),
        out_shape=(
            jax.ShapeDtypeStruct((tokens_dev, wide), jnp.bfloat16),
            jax.ShapeDtypeStruct((length, 2 * width), jnp.bfloat16),
        ),
        in_specs=[smem, smem, vmem, vmem, vmem, vmem],
        out_specs=(vmem, vmem),
        scratch_shapes=[
            pltpu.VMEM((length, heads * block), jnp.float32),
            pltpu.VMEM((length, 2 * width), jnp.float32),
        ],
        compiler_params=pltpu.CompilerParams(vmem_limit_bytes=48 * 1024 * 1024),
        cost_estimate=pl.CostEstimate(
            flops=10 * tokens_dev * wide * length, bytes_accessed=4 * length * wide, transcendentals=0
        ),
    )(table, own, query, out_grad, output, key_value)


def local(query, key, value, out_grad, output, inputs, span_ids):
    tokens_dev, width = key.shape[1], key.shape[2]
    count = lax.axis_size("ctx")
    table = lax.all_gather(span_ids, "ctx", axis=0, tiled=True)
    own_pair = jnp.concatenate([key[0], value[0]], axis=1)
    key_value = lax.all_gather(own_pair, "ctx", axis=0, tiled=True)
    query_low, grads = attention(table, span_ids, query[0], out_grad[0], output[0], key_value, width)
    terms = lax.all_to_all(grads.reshape(count, tokens_dev, 2 * width), "ctx", 0, 0)
    pair = jnp.sum(terms.astype(jnp.float32), axis=0).astype(jnp.bfloat16)
    partial_weights = lax.dot_general(
        inputs[0], pair, (((0,), (0,)), ((), ())), preferred_element_type=jnp.float32
    )
    part = lax.psum_scatter(partial_weights, ("ctx", "dp"), scatter_dimension=0, tiled=True)
    weights = lax.all_gather(part.astype(jnp.bfloat16), ("ctx", "dp"), axis=0, tiled=True)
    weights = weights.astype(jnp.float32)
    return (query_low[None], pair[None, :, :width], pair[None, :, width:], weights)


def solution(mesh):
    row = P("dp", "ctx", None)
    return jax.shard_map(
        local,
        mesh=mesh,
        in_specs=(row, row, row, row, row, row, P("ctx")),
        out_specs=(row, row, row, P()),
        check_vma=False,
    )
```

```python
import functools

import jax
import jax.numpy as jnp
from jax import lax
from jax.experimental import pallas as pl
from jax.experimental.pallas import tpu as pltpu
from jax.sharding import PartitionSpec as P

NEG_FILL = -1e30
LOG2_E = 1.4426950408889634


def dot_nt(left, right):
    return lax.dot_general(left, right, (((1,), (1,)), ((), ())), preferred_element_type=jnp.float32)


def dot_nn(left, right):
    return lax.dot_general(left, right, (((1,), (0,)), ((), ())), preferred_element_type=jnp.float32)


def dot_tn(left, right):
    return lax.dot_general(left, right, (((0,), (0,)), ((), ())), preferred_element_type=jnp.float32)


def attention_kernel(
    chunks, heads, width, block, stride,
    table_ref, own_ref, q_ref, g_ref, o_ref, kv_ref,
    dq_ref, dkv_ref, s_ref, acc_ref,
):
    rows = heads * block
    tokens = 2 * block
    scale = width ** -0.5
    key_row = lax.broadcasted_iota(jnp.int32, (block, rows), 0)
    query_col = lax.rem(lax.broadcasted_iota(jnp.int32, (block, rows), 1), block)
    gap = key_row - query_col
    for slot in range(2):

        def stacked(ref):
            part = ref[slot * block:(slot + 1) * block, :]
            return jnp.concatenate([part[:, h * width:(h + 1) * width] for h in range(heads)], axis=0)

        queries, grads = stacked(q_ref), stacked(g_ref)
        product = grads.astype(jnp.float32) * stacked(o_ref).astype(jnp.float32)
        delta = jnp.sum(jnp.transpose(product), axis=0, keepdims=True) * scale
        own = own_ref[slot]

        def score_step(chunk, high):
            base = pl.multiple_of(chunk * tokens, tokens)
            scores = dot_nt(kv_ref[pl.ds(pl.multiple_of(chunk * stride, 16), tokens), :width], queries) * (scale * LOG2_E)
            for half in range(2):
                ahead = (own - table_ref[2 * chunk + half]) * block
                piece = jnp.where(gap <= ahead, scores[half * block:(half + 1) * block, :], NEG_FILL)
                s_ref[pl.ds(pl.multiple_of(base + half * block, block), block), :] = piece
                high = jnp.maximum(high, jnp.max(piece.reshape(block // 8, 8, rows), axis=0))
            return high

        high = lax.fori_loop(0, chunks, score_step, jnp.full((8, rows), NEG_FILL, jnp.float32))
        top = jnp.max(high, axis=0, keepdims=True)

        def exp_step(chunk, total):
            at = pl.ds(pl.multiple_of(chunk * tokens, tokens), tokens)
            weights = jnp.exp2(s_ref[at, :] - top)
            s_ref[at, :] = weights
            return total + jnp.sum(weights.reshape(tokens // 8, 8, rows), axis=0)

        total = lax.fori_loop(0, chunks, exp_step, jnp.zeros((8, rows), jnp.float32))
        inverse = 1.0 / jnp.sum(total, axis=0, keepdims=True)

        def grad_step(chunk, query_sum):
            at = pl.ds(pl.multiple_of(chunk * tokens, tokens), tokens)
            held = pl.ds(pl.multiple_of(chunk * stride, 16), tokens)
            keys, values = kv_ref[held, :width], kv_ref[held, width:]
            probs = s_ref[at, :] * inverse
            prob_grads = dot_nt(values, grads)
            score_grads = (probs * (prob_grads * scale - delta)).astype(jnp.bfloat16)
            value_add = dot_nn(probs.astype(jnp.bfloat16), grads)
            key_add = dot_nn(score_grads, queries)
            if slot == 0:
                acc_ref[at, :width] = key_add
                acc_ref[at, width:] = value_add
            else:
                dkv_ref[at, :width] = (acc_ref[at, :width] + key_add).astype(jnp.bfloat16)
                dkv_ref[at, width:] = (acc_ref[at, width:] + value_add).astype(jnp.bfloat16)
            return query_sum + dot_tn(keys, score_grads)

        query_sum = lax.fori_loop(0, chunks, grad_step, jnp.zeros((width, rows), jnp.float32))
        for h in range(heads):
            dq_ref[slot * block:(slot + 1) * block, h * width:(h + 1) * width] = jnp.transpose(
                query_sum[:, h * block:(h + 1) * block]
            ).astype(jnp.bfloat16)


def attention(table, own, query, out_grad, output, key_value, width, stride):
    tokens_dev, wide = query.shape
    chunks = key_value.shape[0] // stride
    length = chunks * tokens_dev
    block = tokens_dev // 2
    heads = wide // width
    smem = pl.BlockSpec(memory_space=pltpu.SMEM)
    vmem = pl.BlockSpec(memory_space=pltpu.VMEM)
    return pl.pallas_call(
        functools.partial(attention_kernel, chunks, heads, width, block, stride),
        out_shape=(
            jax.ShapeDtypeStruct((tokens_dev, wide), jnp.bfloat16),
            jax.ShapeDtypeStruct((length, 2 * width), jnp.bfloat16),
        ),
        in_specs=[smem, smem, vmem, vmem, vmem, vmem],
        out_specs=(vmem, vmem),
        scratch_shapes=[
            pltpu.VMEM((length, heads * block), jnp.float32),
            pltpu.VMEM((length, 2 * width), jnp.float32),
        ],
        compiler_params=pltpu.CompilerParams(vmem_limit_bytes=48 * 1024 * 1024),
        cost_estimate=pl.CostEstimate(
            flops=10 * tokens_dev * wide * length, bytes_accessed=4 * length * wide, transcendentals=0
        ),
    )(table, own, query, out_grad, output, key_value)


def local(query, key, value, out_grad, output, inputs, span_ids):
    tokens_dev, width = key.shape[1], key.shape[2]
    count = lax.axis_size("ctx")
    stride = tokens_dev + 16
    numbers = jnp.pad(span_ids.astype(jnp.bfloat16)[None, :], ((0, 15), (0, 2 * width - 2)))
    own_pair = jnp.concatenate([jnp.concatenate([key[0], value[0]], axis=1), numbers], axis=0)
    key_value = lax.all_gather(own_pair, "ctx", axis=0, tiled=True)
    table = key_value.reshape(count, stride, 2 * width)[:, tokens_dev, :2].astype(jnp.int32).reshape(-1)
    query_low, grads = attention(
        table, span_ids, query[0], out_grad[0], output[0], key_value, width, stride
    )
    terms = lax.all_to_all(grads.reshape(count, tokens_dev, 2 * width), "ctx", 0, 0)
    pair = jnp.sum(terms.astype(jnp.float32), axis=0).astype(jnp.bfloat16)
    partial_weights = lax.dot_general(
        inputs[0], pair, (((0,), (0,)), ((), ())), preferred_element_type=jnp.float32
    )
    weights = lax.psum(partial_weights, ("ctx", "dp"))
    return (query_low[None], pair[None, :, :width], pair[None, :, width:], weights)


def solution(mesh):
    row = P("dp", "ctx", None)
    return jax.shard_map(
        local,
        mesh=mesh,
        in_specs=(row, row, row, row, row, row, P("ctx")),
        out_specs=(row, row, row, P()),
        check_vma=False,
    )
```
